32 devices in a mesh: groups: 2 (over x), tgt: 8 (over z, y), tile: 2 (over core).
Axes of the slice: x: 2, y: 2, z: 4, core: 2. Of those that a mesh axis runs over, the one named last changes fastest.
Arguments:
- embeddings: bfloat16 [53248, 1024], P(('groups', 'tile'), 'tgt'), parts along dimension 0, may hold values from -6 to 6
- land_mask: int32 [53248], P(('groups', 'tile')), parts along dimension 0, may hold values from 0 to 1, as said below
- factor_in: bfloat16 [1024, 256], P('tgt'), may hold values from -0.1875 to 0.1875
- factor_out: bfloat16 [256, 4096], P(None, 'tgt'), may hold values from -0.375 to 0.375
- targets: bfloat16 [53248, 4096], P(('groups', 'tile'), 'tgt'), parts along dimension 0, may hold values from -6 to 6
- target_weight: float32 [4096], P('tgt'), may hold values from 64 to 256
Outputs:
- grad_in: float32 [2048, 256], P(('groups', 'tgt'), 'tile'), parts along dimension 0
- grad_out: float32 [512, 4096], P(('groups', 'tile'), 'tgt'), parts along dimension 0
The draws below stay inside these ranges and needn't reach their ends.
There are 2 independent parts, one for each index of `groups`. The reference program is written for one: setup_inputs(seed, part) draws one part's arguments, and reference() takes and returns one part's arrays. A program takes and returns all parts, laid end to end along the dimension named above; an argument that names none is the same for every part. Nothing has to cross between parts.
Inputs may be any that keep to these rules, and one draw needn't show every extreme that they name: `land_mask`: 1 marks a land cell.
All inputs are finite; a program needn't handle non-finite values.
Results may differ from the reference program's by a relative error of at most 0.0012.
Values may be sent and summed in bfloat16 or wider, within the bound.
No kernel may reach another device: no remote copies, remote signals or barrier semaphores. Data moves between devices by JAX's collectives and lax.ppermute only.
A program may use at most 128 MiB of HBM per device.

```python
import math
import jax
import jax.numpy as jnp

E = 1024
R = 256
K = 4096
CELLS = 26624


def draw_land_mask(key, part):
    position = jnp.arange(CELLS, dtype=jnp.int32)
    thresh_level = jnp.where(position >= CELLS // 2, 3, 1).astype(jnp.int32)
    picked = jax.random.randint(key, (CELLS,), 0, 4, dtype=jnp.int32)
    return jnp.where(picked < thresh_level, 1, 0).astype(jnp.int32)


def levels(rng, dims, split, smallest, high):
    def one(dim, parts):
        draws = jax.random.uniform(jax.random.fold_in(jax.random.fold_in(rng, 6), dim), (parts,), jnp.float32, smallest / len(split), high / len(split))
        return jnp.repeat(jnp.exp(draws), dims[dim] // parts).reshape((-1,) + (1,) * (len(dims) - dim - 1))

    factor_of = one(*split[0])
    for cut in split[1:]:
        factor_of = factor_of * one(*cut)
    return factor_of


def centred(own_key, shape, deviation, limit, shards=(), kind=jnp.bfloat16):
    entries = deviation * jax.random.normal(own_key, shape, jnp.float32)
    if shards:
        entries = entries * levels(own_key, shape, shards, -0.22, 0.18)
    return jnp.clip(entries, -limit, limit).astype(kind)


def setup_inputs(seed: int = 0, part: int = 0) -> dict:
    keys = jax.random.split(jax.random.key(seed), 7)
    own_keys = jax.random.split(jax.random.fold_in(keys[6], part), 7)
    return {
        "embeddings": centred(own_keys[0], (CELLS, E), 1.0, 6.0, ((0, 2), (1, 8))),
        "land_mask": draw_land_mask(jax.random.fold_in(jax.random.fold_in(keys[6], part), 71), part),
        "factor_in": centred(keys[2], (E, R), E ** -0.5, 0.1875, ((0, 8),)),
        "factor_out": centred(keys[3], (R, K), R ** -0.5, 0.375, ((1, 8),)),
        "targets": centred(own_keys[4], (CELLS, K), 1.0, 6.0, ((0, 2), (1, 8))),
        "target_weight": jnp.clip(jnp.exp(math.log(256.0) - 1.3862944 * jax.random.uniform(keys[5], (K,), jnp.float32) ** levels(keys[5], (K,), ((0, 8),), -0.2, 0.2)), 64.0, 256.0),
    }


def reference(embeddings, land_mask, factor_in, factor_out, targets, target_weight):
    latent = jnp.dot(embeddings, factor_in, preferred_element_type=jnp.float32).astype(jnp.bfloat16)
    predicted = jnp.dot(latent, factor_out, preferred_element_type=jnp.float32)
    land_total = jnp.sum(land_mask).astype(jnp.float32)
    cell_weight = land_mask.astype(jnp.float32) / land_total
    residual = ((predicted - targets.astype(jnp.float32)) * cell_weight[:, None] * target_weight[None, :]).astype(jnp.bfloat16)
    grad_out = jnp.dot(latent.T, residual, preferred_element_type=jnp.float32)
    latent_grad = jnp.dot(residual, factor_out.T, preferred_element_type=jnp.float32).astype(jnp.bfloat16)
    grad_in = jnp.dot(embeddings.T, latent_grad, preferred_element_type=jnp.float32)
    return (grad_in, grad_out)
```

```python
import functools

import jax
import jax.numpy as jnp
from jax import lax
from jax.experimental import pallas as pl
from jax.experimental.pallas import tpu as pltpu
from jax.sharding import PartitionSpec as P

BF16 = jnp.bfloat16
F32 = jnp.float32
BLOCK = 256
SUB = 16


def compact_kernel(cap, rows, mask_ref, x_ref, out_ref, offset):
    step = pl.program_id(0)

    @pl.when(step == 0)
    def _():
        count = jnp.sum(mask_ref[...])
        base = jnp.maximum(cap - count, 0)
        offset[0] = base

        def clear(i, carry):
            out_ref[pl.ds(pl.multiple_of(i * BLOCK, BLOCK), BLOCK), :] = jnp.zeros(
                (BLOCK, out_ref.shape[1]), out_ref.dtype
            )
            return carry

        lax.fori_loop(0, base // BLOCK + 1, clear, 0)

    first = offset[0]
    mask = mask_ref[pl.ds(step, 1), 0, :]
    offset[0] = first + jnp.sum(mask)
    start = jnp.minimum(first // SUB * SUB, rows - BLOCK - SUB)
    start = pl.multiple_of(start, SUB)
    before = lax.broadcasted_iota(jnp.int32, (BLOCK, BLOCK), 0) < lax.broadcasted_iota(
        jnp.int32, (BLOCK, BLOCK), 1
    )
    prefix = jnp.dot(
        mask.astype(F32).astype(BF16), before.astype(F32).astype(BF16), preferred_element_type=F32
    ).astype(jnp.int32)
    slot = jnp.where(mask > 0, prefix + (first - start), -1)
    choose = lax.broadcasted_iota(jnp.int32, (BLOCK + SUB, BLOCK), 0) == slot
    moved = jnp.dot(choose.astype(F32).astype(BF16), x_ref[...], preferred_element_type=F32).astype(BF16)
    out_ref[pl.ds(start, SUB), :] += moved[:SUB]
    out_ref[pl.ds(start + SUB, BLOCK), :] = moved[SUB:]


def compact(mask_blocks, x, cap, extra):
    blocks, width = mask_blocks.shape[0], x.shape[1]
    rows = cap + extra + 2 * BLOCK
    return pl.pallas_call(
        functools.partial(compact_kernel, cap, rows),
        grid=(blocks,),
        out_shape=jax.ShapeDtypeStruct((rows, width), x.dtype),
        in_specs=[
            pl.BlockSpec(mask_blocks.shape, lambda i: (0, 0, 0)),
            pl.BlockSpec((BLOCK, width), lambda i: (i, 0)),
        ],
        out_specs=pl.BlockSpec((rows, width), lambda i: (0, 0)),
        scratch_shapes=[pltpu.SMEM((1,), jnp.int32)],
        compiler_params=pltpu.CompilerParams(vmem_limit_bytes=40 * 1024 * 1024),
        cost_estimate=pl.CostEstimate(
            flops=2 * (BLOCK + SUB) * x.shape[0] * width,
            bytes_accessed=2 * (x.shape[0] + rows) * width,
            transcendentals=0,
        ),
    )(mask_blocks, x)


def balance(buffer, cap, extra, received):
    other = lax.ppermute(buffer[cap : cap + extra], "tile", [(0, 1), (1, 0)])
    row = lax.broadcasted_iota(jnp.int32, (extra, 1), 0)
    head = jnp.where(row < received, other, buffer[:extra])
    return jnp.concatenate([head, buffer[extra:cap]], axis=0)


def gradients(cells, targets, factor_in, factor_out, target_weight, land_total):
    shards = lax.axis_size("tgt")
    own_cells = lax.all_to_all(cells, "tgt", split_axis=0, concat_axis=1, tiled=True)
    whole_in = lax.all_gather(factor_in, "tgt", axis=0, tiled=True)
    own_latent = jnp.dot(own_cells, whole_in, preferred_element_type=F32).astype(BF16)
    latent = lax.all_gather(own_latent, "tgt", axis=0, tiled=True)
    predicted = jnp.dot(latent, factor_out, preferred_element_type=F32)
    residual = (
        (predicted - targets.astype(F32)) * (1.0 / land_total) * target_weight[None, :]
    ).astype(BF16)
    out_partial = jnp.einsum("pr,pk->rk", latent, residual, preferred_element_type=F32)
    grad_out = lax.psum_scatter(out_partial, "tile", scatter_dimension=0, tiled=True)
    terms = jnp.einsum("pk,rk->pr", residual, factor_out, preferred_element_type=F32).astype(BF16)
    parts = lax.all_to_all(
        terms.reshape(shards, -1, terms.shape[1]), "tgt", split_axis=0, concat_axis=0, tiled=True
    )
    latent_grad = jnp.sum(parts.astype(F32), axis=0).astype(BF16)
    in_partial = jnp.einsum("pe,pr->er", own_cells, latent_grad, preferred_element_type=F32)
    in_half = lax.psum_scatter(in_partial, "tile", scatter_dimension=1, tiled=True)
    grad_in = lax.psum_scatter(in_half, "tgt", scatter_dimension=0, tiled=True)
    return grad_in, grad_out


def local(embeddings, land_mask, factor_in, factor_out, targets, target_weight):
    cells = embeddings.shape[0]
    shards, tiles, groups = lax.axis_size("tgt"), lax.axis_size("tile"), lax.axis_size("groups")
    grain = SUB * shards * 2
    cap = -(-cells * 33 // (64 * grain)) * grain
    extra = cap // 2

    tile, group = lax.axis_index("tile"), lax.axis_index("groups")
    count = jnp.sum(land_mask)
    place = jnp.arange(groups * tiles, dtype=jnp.int32)
    counts = lax.psum(
        jnp.where(place == group * tiles + tile, count, 0), ("groups", "tile")
    ).reshape(groups, tiles)
    over = jnp.maximum(counts - cap, 0)
    fits = jnp.all((over <= extra) & (jnp.minimum(counts, cap) + over[:, ::-1] <= cap))
    mine = lax.dynamic_index_in_dim(counts, group, 0, keepdims=False)
    land_total = jnp.sum(mine).astype(F32)
    received = lax.dynamic_index_in_dim(
        lax.dynamic_index_in_dim(over, group, 0, keepdims=False), 1 - tile, 0, keepdims=False
    )
    mask_blocks = land_mask.reshape(-1, 1, BLOCK)

    def compacted():
        few = balance(compact(mask_blocks, embeddings, cap, extra), cap, extra, received)
        few_targets = balance(compact(mask_blocks, targets, cap, extra), cap, extra, received)
        return gradients(few, few_targets, factor_in, factor_out, target_weight, land_total)

    def full():
        land = land_mask[:, None] > 0
        return gradients(
            jnp.where(land, embeddings, 0), jnp.where(land, targets, 0),
            factor_in, factor_out, target_weight, land_total,
        )

    return lax.cond(fits, compacted, full)


def solution(mesh):
    return jax.shard_map(
        local,
        mesh=mesh,
        in_specs=(
            P(("groups", "tile"), "tgt"),
            P(("groups", "tile")),
            P("tgt", None),
            P(None, "tgt"),
            P(("groups", "tile"), "tgt"),
            P("tgt"),
        ),
        out_specs=(P(("groups", "tgt"), "tile"), P(("groups", "tile"), "tgt")),
        check_vma=False,
    )
```

```python
import functools

import jax
import jax.numpy as jnp
from jax import lax
from jax.experimental import pallas as pl
from jax.experimental.pallas import tpu as pltpu
from jax.sharding import PartitionSpec as P

BF16 = jnp.bfloat16
F32 = jnp.float32
BLOCK = 256
GROUP = 13
SUB = 16
CHUNKS = 2
MIB = 1024 * 1024


def dot(a, b, dims=((1,), (0,))):
    return lax.dot_general(a, b, (dims, ((), ())), preferred_element_type=F32)


def compact_kernel(group, cap, extra, rows, shards, first_ref, pair_ref, mask_ref, cells_ref, targets_ref, *refs):
    (late_ref, early_ref, over_ref, main_ref, pair_out_ref, far_ref, cells_all, targets_all, sems) = refs
    step = pl.program_id(0)
    arrays = ((cells_ref, cells_all), (targets_ref, targets_all))

    @pl.when(step == 0)
    def _():
        def clear(i, carry):
            for _, out_ref in arrays:
                out_ref[pl.ds(pl.multiple_of(i * BLOCK, BLOCK), BLOCK), :] = jnp.zeros(
                    (BLOCK, out_ref.shape[1]), out_ref.dtype
                )
            return carry

        lax.fori_loop(0, first_ref[0] // BLOCK + 1, clear, 0)

    before = lax.broadcasted_iota(jnp.int32, (BLOCK, BLOCK), 0) < lax.broadcasted_iota(
        jnp.int32, (BLOCK, BLOCK), 1
    )
    before = before.astype(F32).astype(BF16)
    place = lax.broadcasted_iota(jnp.int32, (BLOCK + SUB, BLOCK), 0)
    mask = mask_ref[0]
    prefix = dot(mask.astype(F32).astype(BF16), before).astype(jnp.int32)
    for k in range(group):
        first = first_ref[step * group + k]
        start = jnp.minimum(first // SUB * SUB, rows - BLOCK - SUB)
        slot = jnp.where(mask[k : k + 1] > 0, prefix[k : k + 1] + (first - start), -1)
        choose = (place == slot).astype(F32).astype(BF16)
        start = pl.multiple_of(start, SUB)
        for x_ref, out_ref in arrays:
            moved = dot(choose, x_ref[k * BLOCK : (k + 1) * BLOCK, :]).astype(BF16)
            out_ref[pl.ds(start, SUB), :] += moved[:SUB]
            out_ref[pl.ds(start + SUB, BLOCK), :] = moved[SUB:]

    @pl.when(step == pl.num_programs(0) - 1)
    def _():
        block, count = extra // shards, shards // 2
        moves = [
            (cells_all.at[pl.ds(extra + (y * count + z) * block, block)], late_ref.at[2 * z + y])
            for z in range(count)
            for y in (0, 1)
        ]
        moves += [
            (cells_all.at[pl.ds(cap, extra)], over_ref),
            (cells_all.at[pl.ds(0, extra)], early_ref),
            (targets_all.at[pl.ds(pl.multiple_of(pair_ref[0], SUB), extra // 2)], pair_out_ref),
            (targets_all.at[pl.ds(cap, extra)], far_ref),
            (targets_all.at[pl.ds(0, cap)], main_ref),
        ]
        copies = [pltpu.make_async_copy(x, out, sems.at[i]) for i, (x, out) in enumerate(moves)]
        for copy in copies:
            copy.start()
        for copy in copies:
            copy.wait()


def compact(firsts, pair_at, mask_blocks, cells, targets, cap, extra, shards):
    rows = -(-(cap + extra + 2 * BLOCK) // BLOCK) * BLOCK
    blocks = mask_blocks.shape[0]
    group = max(g for g in range(1, GROUP + 1) if blocks % g == 0)
    width, columns = cells.shape[1], targets.shape[1]
    shapes = [(shards, extra // shards, width), (extra, width), (extra, width)]
    shapes += [(cap, columns), (extra // 2, columns), (extra, columns)]
    return pl.pallas_call(
        functools.partial(compact_kernel, group, cap, extra, rows, shards),
        grid_spec=pltpu.PrefetchScalarGridSpec(
            num_scalar_prefetch=2,
            grid=(blocks // group,),
            in_specs=[pl.BlockSpec((1, group, BLOCK), lambda i, f, p: (i, 0, 0))]
            + [pl.BlockSpec((group * BLOCK, w), lambda i, f, p: (i, 0)) for w in (width, columns)],
            out_specs=[pl.BlockSpec(memory_space=pl.ANY)] * len(shapes),
            scratch_shapes=[
                pltpu.VMEM((rows, width), BF16),
                pltpu.VMEM((rows, columns), BF16),
                pltpu.SemaphoreType.DMA((shards + 5,)),
            ],
        ),
        out_shape=[jax.ShapeDtypeStruct(shape, BF16) for shape in shapes],
        compiler_params=pltpu.CompilerParams(vmem_limit_bytes=40 * MIB),
        cost_estimate=pl.CostEstimate(
            flops=2 * (BLOCK + SUB) * blocks * BLOCK * (width + columns),
            bytes_accessed=2 * (blocks * BLOCK + rows) * (width + columns),
            transcendentals=0,
        ),
        name="compact",
    )(firsts, pair_at.reshape(1), mask_blocks.reshape(-1, group, BLOCK), cells, targets)


SWAP = [(0, 1), (1, 0)]


def send(x, moves):
    return lax.ppermute(x, "tgt", moves)


def shifted(count, s, flip):
    return [(2 * z + y, 2 * ((z + s) % count) + (y ^ flip)) for z in range(count) for y in (0, 1)]


def latent_kernel(y_ref, slot_ref, cells_ref, factor_ref, out_ref):
    total = None
    for source in range(cells_ref.shape[0]):
        flip = (y_ref[0] + source) % 2
        part = dot(cells_ref[source], factor_ref[flip, slot_ref[source // 2]])
        total = part if total is None else total + part
    out_ref[...] = total.astype(BF16)


def latent_of(y, slot_of, cells, factor_in):
    sources, rows, width = cells.shape
    rank = factor_in.shape[3]
    return pl.pallas_call(
        latent_kernel,
        in_specs=[pl.BlockSpec(memory_space=pltpu.SMEM)] * 2 + [pl.BlockSpec(memory_space=pltpu.VMEM)] * 2,
        out_specs=pl.BlockSpec(memory_space=pltpu.VMEM),
        out_shape=jax.ShapeDtypeStruct((rows, rank), BF16),
        compiler_params=pltpu.CompilerParams(vmem_limit_bytes=16 * MIB),
        cost_estimate=pl.CostEstimate(
            flops=2 * sources * rows * width * rank,
            bytes_accessed=2 * sources * width * (rows + rank) + 2 * rows * rank,
            transcendentals=0,
        ),
        name="latent",
    )(y.reshape(1), slot_of, cells, factor_in)


def residual_kernel(
    count, mixed, own_ref, pair_ref, part_ref, scale_ref, weight_ref, far_weight_ref, factor_ref, far_factor_ref, *refs
):
    slot = pl.program_id(0)
    latents, refs = refs[:count], refs[count:]
    targets_ref, far_targets_ref, refs = refs[0], refs[1], refs[2:]
    if mixed:
        other_ref, refs = refs[0], refs[1:]
    terms, (out_ref, far_out_ref, held) = refs[:count], refs[count:]
    rows = targets_ref.shape[0]

    for s in range(count):

        @pl.when(slot == s)
        def _():
            held[...] = latents[s][...]

    @pl.when(slot == 0)
    def _():
        out_ref[...] = jnp.zeros_like(out_ref)
        far_out_ref[...] = jnp.zeros_like(far_out_ref)

    latent = held[...]
    targets = targets_ref[...].astype(F32)
    if mixed:
        row = own_ref[slot] * rows + lax.broadcasted_iota(jnp.int32, (rows, 1), 0)
        targets = jnp.where(row < part_ref[0], other_ref[...].astype(F32), targets)
    factor, far_factor = factor_ref[...], far_factor_ref[...]
    scale = scale_ref[0, 0]
    residual = ((dot(latent, factor) - targets) * scale * weight_ref[...]).astype(BF16)
    far_targets = far_targets_ref[...].astype(F32)
    far_residual = ((dot(latent, far_factor) - far_targets) * scale * far_weight_ref[...]).astype(BF16)
    total = dot(residual, factor, ((1,), (1,))) + dot(far_residual, far_factor, ((1,), (1,)))
    total = total.astype(BF16)
    for s in range(count):

        @pl.when(slot == s)
        def _():
            terms[s][...] = total

    out_ref[...] += dot(latent, residual, ((0,), (0,)))
    far_out_ref[...] += dot(latent, far_residual, ((0,), (0,)))


def residual_of(own_at, pair_at, received, scale, weights, factors, latents, own, pair, other):
    count = len(latents)
    rows, rank = latents[0].shape
    width = own.shape[1]
    mixed = other is not None
    whole = lambda shape: pl.BlockSpec(shape, lambda i, o, p, r: (0, 0))
    by_own = pl.BlockSpec((rows, width), lambda i, o, p, r: (o[i], 0))
    by_pair = pl.BlockSpec((rows, width), lambda i, o, p, r: (p[i], 0))
    result = pl.pallas_call(
        functools.partial(residual_kernel, count, mixed),
        grid_spec=pltpu.PrefetchScalarGridSpec(
            num_scalar_prefetch=3,
            grid=(count,),
            in_specs=[pl.BlockSpec((1, 1), lambda i, o, p, r: (0, 0), memory_space=pltpu.SMEM)]
            + [whole((1, width))] * 2
            + [whole((rank, width))] * 2
            + [whole((rows, rank))] * count
            + [by_own, by_pair]
            + [by_own] * mixed,
            out_specs=[whole((rows, rank))] * count + [whole((rank, width))] * 2,
            scratch_shapes=[pltpu.VMEM((rows, rank), BF16)],
        ),
        out_shape=[jax.ShapeDtypeStruct((rows, rank), BF16)] * count
        + [jax.ShapeDtypeStruct((rank, width), F32)] * 2,
        compiler_params=pltpu.CompilerParams(vmem_limit_bytes=56 * MIB),
        cost_estimate=pl.CostEstimate(
            flops=count * rows * rank * width,
            bytes_accessed=count * rows * (rank + width),
            transcendentals=0,
        ),
        name="residual",
    )(
        own_at, pair_at, received, scale.reshape(1, 1), *[w.reshape(1, -1) for w in weights], *factors,
        *latents, own, pair, *([other] * mixed),
    )
    return result[:count], result[count], result[count + 1]


def in_kernel(tile_ref, *refs):
    (keep_ref, pass_ref), refs = refs[-2:], refs[:-2]
    half = keep_ref.shape[2]
    for tile in (0, 1):

        @pl.when(tile_ref[0] == tile)
        def _():
            for source in range(keep_ref.shape[0]):
                total = None
                for cells_ref, grads_ref in zip(refs[:CHUNKS], refs[CHUNKS:]):
                    part = dot(cells_ref[source], grads_ref[...], ((0,), (0,)))
                    total = part if total is None else total + part
                keep_ref[source] = total[:, tile * half : (tile + 1) * half]
                pass_ref[source] = total[:, (1 - tile) * half : (2 - tile) * half]


def in_of(tile, cells, latent_grads):
    sources, rows, width = cells[0].shape
    rank = latent_grads[0].shape[1]
    shape = jax.ShapeDtypeStruct((sources, width, rank // 2), F32)
    return pl.pallas_call(
        in_kernel,
        in_specs=[pl.BlockSpec(memory_space=pltpu.SMEM)]
        + [pl.BlockSpec(memory_space=pltpu.VMEM)] * (2 * CHUNKS),
        out_specs=[pl.BlockSpec(memory_space=pltpu.VMEM)] * 2,
        out_shape=[shape, shape],
        compiler_params=pltpu.CompilerParams(vmem_limit_bytes=16 * MIB),
        cost_estimate=pl.CostEstimate(
            flops=2 * CHUNKS * sources * rows * width * rank,
            bytes_accessed=2 * CHUNKS * rows * (width * sources + rank) + 4 * sources * width * rank,
            transcendentals=0,
        ),
        name="in_part",
    )(tile.reshape(1), *cells, *latent_grads)


def compacted_gradients(
    late, early, over, own_targets, pair_late, over_targets, received, whole_in, factors, weights, land_total
):
    shards = lax.axis_size("tgt")
    count = shards // 2
    index, tile = lax.axis_index("tgt"), lax.axis_index("tile")
    z, y = index // 2, index % 2
    extra = early.shape[0]
    scale = 1.0 / land_total
    slot_z = (z - jnp.arange(count, dtype=jnp.int32)) % count

    other_cells = lax.ppermute(over, "tile", SWAP)
    other_targets = lax.ppermute(over_targets, "tile", SWAP)

    def merged(own, other, at, size):
        row = at + lax.broadcasted_iota(jnp.int32, (size, 1), 0)
        own, other = (lax.dynamic_slice_in_dim(x, at, size, axis=0) for x in (own, other))
        return jnp.where(row < received[0], other, own)

    order = (1, 0)
    early = merged(early, other_cells, 0, extra)
    early = early.reshape(2, count, extra // shards, -1).swapaxes(0, 1).reshape(late.shape)

    def owners_cells(x):
        return lax.all_to_all(x, "tgt", split_axis=0, concat_axis=0, tiled=True)

    def along_line(x):
        return [x] + [send(x, shifted(count, s, 0)) for s in range(1, count)]

    pairs = {1: send(pair_late, shifted(count, 0, 1))}
    cells = {1: owners_cells(late), 0: owners_cells(early)}
    mine = latent_of(y, slot_z, cells[1], whole_in)
    mine, own_targets, other_targets = lax.optimization_barrier((mine, own_targets, other_targets))
    latents = {1: along_line(mine)}
    pair_early = merged(own_targets, other_targets, (1 - y) * (extra // 2), extra // 2)
    pairs[0] = send(pair_early, shifted(count, 0, 1))
    cells[0], latents[1] = lax.optimization_barrier((cells[0], latents[1]))
    latents[0] = along_line(latent_of(y, slot_z, cells[0], whole_in))

    def residual(chunk):
        return residual_of(
            slot_z + (chunk * 2 + y) * count, slot_z, received, scale, weights, factors,
            latents[chunk], own_targets, pairs[chunk], other_targets if chunk == 0 else None,
        )

    def summed(terms):
        total = terms[0].astype(F32)
        for s in range(1, count):
            total = total + send(terms[s], shifted(count, -s, 0)).astype(F32)
        return total.astype(BF16)

    late_parts, latents[0], pairs[0] = lax.optimization_barrier((residual(1), latents[0], pairs[0]))
    grads = {1: summed(late_parts[0])}
    early_parts, grads[1] = lax.optimization_barrier((residual(0), grads[1]))
    grads[0] = summed(early_parts[0])
    own_part, far_part = late_parts[1] + early_parts[1], late_parts[2] + early_parts[2]
    out_part = jnp.stack([own_part, far_part])
    half = out_part.shape[1] // 2
    out_half = lax.dynamic_slice_in_dim(out_part, tile * half, half, axis=1) + lax.ppermute(
        lax.dynamic_slice_in_dim(out_part, (1 - tile) * half, half, axis=1), "tile", SWAP
    )
    grad_out = out_half[0] + send(out_half[1], shifted(count, 0, 1))
    grads[0], grad_out = lax.optimization_barrier((grads[0], grad_out))
    keep, passed = in_of(tile, [cells[c] for c in order], [grads[c] for c in order])
    mine = keep + lax.ppermute(passed, "tile", SWAP)
    grad_in = lax.dynamic_index_in_dim(mine, index, 0, keepdims=False)
    for s in range(1, shards):
        to_z, to_y = (z + s) % count, y ^ (s // count)
        part = lax.dynamic_index_in_dim(mine, 2 * to_z + to_y, 0, keepdims=False)
        grad_in = grad_in + send(part, shifted(count, s % count, s // count))
    return grad_in, grad_out


def full_gradients(cells, targets, factor_in, factor_out, target_weight, land_total):
    shards = lax.axis_size("tgt")
    own_cells = lax.all_to_all(cells, "tgt", split_axis=0, concat_axis=1, tiled=True)
    whole_in = lax.all_gather(factor_in, "tgt", axis=0, tiled=True)
    own_latent = dot(own_cells, whole_in).astype(BF16)
    latent = lax.all_gather(own_latent, "tgt", axis=0, tiled=True)
    residual = (
        (dot(latent, factor_out) - targets.astype(F32)) * (1.0 / land_total) * target_weight[None, :]
    ).astype(BF16)
    out_partial = dot(latent, residual, ((0,), (0,)))
    grad_out = lax.psum_scatter(out_partial, "tile", scatter_dimension=0, tiled=True)
    terms = dot(residual, factor_out, ((1,), (1,))).astype(BF16)
    parts = lax.all_to_all(
        terms.reshape(shards, -1, terms.shape[1]), "tgt", split_axis=0, concat_axis=0, tiled=True
    )
    latent_grad = jnp.sum(parts.astype(F32), axis=0).astype(BF16)
    in_partial = dot(own_cells, latent_grad, ((0,), (0,)))
    in_half = lax.psum_scatter(in_partial, "tile", scatter_dimension=1, tiled=True)
    grad_in = lax.psum_scatter(in_half, "tgt", scatter_dimension=0, tiled=True)
    return grad_in, grad_out


def local(embeddings, land_mask, factor_in, factor_out, targets, target_weight):
    cells = embeddings.shape[0]
    shards, groups = lax.axis_size("tgt"), lax.axis_size("groups")
    grain = SUB * shards * CHUNKS
    cap = -(-cells * 33 // (64 * grain)) * grain
    extra = cap // 2

    y = lax.axis_index("tgt") % 2
    pair_in = jnp.stack([factor_in, send(factor_in, shifted(shards // 2, 0, 1))])
    weights = (target_weight, send(target_weight, shifted(shards // 2, 0, 1)))
    mask_blocks = land_mask.reshape(-1, BLOCK)
    in_block = jnp.sum(mask_blocks, axis=1)
    land = jnp.sum(land_mask).reshape(1)
    at = jnp.arange(in_block.shape[0], dtype=jnp.int32)
    firsts = jnp.maximum(cap - land, 0) + jnp.sum(
        jnp.where(at[None, :] < at[:, None], in_block[None, :], 0), axis=1
    )
    other = lax.ppermute(land, "tile", SWAP)
    firsts, mask_blocks, other, pair_in = lax.optimization_barrier((firsts, mask_blocks, other, pair_in))
    counts = [jnp.concatenate([land, other])]
    counts += [
        lax.ppermute(counts[0], "groups", [(a, (a + g) % groups) for a in range(groups)]) for g in range(1, groups)
    ]
    line_in = [pair_in] + [send(pair_in, shifted(shards // 2, s, 0)) for s in range(1, shards // 2)]
    factors = (factor_out, send(factor_out, shifted(shards // 2, 0, 1)))
    kept = compact(firsts, extra + (1 - y) * (extra // 2), mask_blocks, embeddings, targets, cap, extra, shards)
    kept, counts, line_in, factors = lax.optimization_barrier((kept, counts, line_in, factors))
    counts = jnp.stack(counts)
    low, high = jnp.min(counts, axis=1), jnp.max(counts, axis=1)
    fits = jnp.all((low + jnp.maximum(high - cap, 0) <= cap) & (high - cap <= extra))
    land_total = (land + other)[0].astype(F32)
    received = jnp.maximum(other - cap, 0)

    def few():
        return compacted_gradients(
            *kept, received, jnp.stack(line_in, axis=1), factors, weights, land_total
        )

    def full():
        is_land = land_mask[:, None] > 0
        return full_gradients(
            jnp.where(is_land, embeddings, 0), jnp.where(is_land, targets, 0),
            factor_in, factor_out, target_weight, land_total,
        )

    return lax.cond(fits, few, full)


def solution(mesh):
    return jax.shard_map(
        local,
        mesh=mesh,
        in_specs=(
            P(("groups", "tile"), "tgt"),
            P(("groups", "tile")),
            P("tgt", None),
            P(None, "tgt"),
            P(("groups", "tile"), "tgt"),
            P("tgt"),
        ),
        out_specs=(P(("groups", "tgt"), "tile"), P(("groups", "tile"), "tgt")),
        check_vma=False,
    )
```

```python
import functools

import jax
import jax.numpy as jnp
from jax import lax
from jax.experimental import pallas as pl
from jax.experimental.pallas import tpu as pltpu
from jax.sharding import PartitionSpec as P

BF16 = jnp.bfloat16
F32 = jnp.float32
BLOCK = 256
GROUP = 13
SUB = 16
CHUNKS = 2
MIB = 1024 * 1024


def dot(a, b, dims=((1,), (0,))):
    return lax.dot_general(a, b, (dims, ((), ())), preferred_element_type=F32)


def compact_kernel(
    group, cap, extra, rows, shards, known, first_ref, pair_ref, mask_ref, cells_ref, targets_ref, *refs
):
    counts, refs = [ref[0] for ref in refs[:known]], refs[known:]
    (facts_ref, late_ref, early_ref, over_ref, main_ref, pair_out_ref, far_ref, cells_all, targets_all, sems) = refs
    step = pl.program_id(0)
    arrays = ((cells_ref, cells_all), (targets_ref, targets_all))

    @pl.when(step == 0)
    def _():
        fits = jnp.int32(1)
        for one, two in zip(counts[::2], counts[1::2]):
            low, high = jnp.minimum(one, two), jnp.maximum(one, two)
            fits = jnp.where((low + jnp.maximum(high - cap, 0) <= cap) & (high - cap <= extra), fits, 0)
        facts_ref[0] = fits
        facts_ref[1] = jnp.maximum(counts[1] - cap, 0)
        facts_ref[2] = counts[0] + counts[1]

        def clear(i, carry):
            for _, out_ref in arrays:
                out_ref[pl.ds(pl.multiple_of(i * BLOCK, BLOCK), BLOCK), :] = jnp.zeros(
                    (BLOCK, out_ref.shape[1]), out_ref.dtype
                )
            return carry

        lax.fori_loop(0, first_ref[0] // BLOCK + 1, clear, 0)

    before = lax.broadcasted_iota(jnp.int32, (BLOCK, BLOCK), 0) < lax.broadcasted_iota(
        jnp.int32, (BLOCK, BLOCK), 1
    )
    before = before.astype(F32).astype(BF16)
    place = lax.broadcasted_iota(jnp.int32, (BLOCK + SUB, BLOCK), 0)
    mask = mask_ref[0]
    prefix = dot(mask.astype(F32).astype(BF16), before).astype(jnp.int32)
    for k in range(group):
        first = first_ref[step * group + k]
        start = jnp.minimum(first // SUB * SUB, rows - BLOCK - SUB)
        slot = jnp.where(mask[k : k + 1] > 0, prefix[k : k + 1] + (first - start), -1)
        choose = (place == slot).astype(F32).astype(BF16)
        start = pl.multiple_of(start, SUB)
        for x_ref, out_ref in arrays:
            moved = dot(choose, x_ref[k * BLOCK : (k + 1) * BLOCK, :]).astype(BF16)
            out_ref[pl.ds(start, SUB), :] += moved[:SUB]
            out_ref[pl.ds(start + SUB, BLOCK), :] = moved[SUB:]

    @pl.when(step == pl.num_programs(0) - 1)
    def _():
        block, count = extra // shards, shards // 2
        moves = [
            (cells_all.at[pl.ds(extra + (y * count + z) * block, block)], late_ref.at[2 * z + y])
            for z in range(count)
            for y in (0, 1)
        ]
        moves += [
            (cells_all.at[pl.ds(cap, extra)], over_ref),
            (cells_all.at[pl.ds(0, extra)], early_ref),
            (targets_all.at[pl.ds(pl.multiple_of(pair_ref[0], SUB), extra // 2)], pair_out_ref),
            (targets_all.at[pl.ds(cap, extra)], far_ref),
            (targets_all.at[pl.ds(0, cap)], main_ref),
        ]
        copies = [pltpu.make_async_copy(x, out, sems.at[i]) for i, (x, out) in enumerate(moves)]
        for copy in copies:
            copy.start()
        for copy in copies:
            copy.wait()


def compact(firsts, pair_at, mask_blocks, cells, targets, counts, cap, extra, shards):
    rows = -(-(cap + extra + 2 * BLOCK) // BLOCK) * BLOCK
    blocks = mask_blocks.shape[0]
    group = max(g for g in range(1, GROUP + 1) if blocks % g == 0)
    width, columns = cells.shape[1], targets.shape[1]
    shapes = [(shards, extra // shards, width), (extra, width), (extra, width)]
    shapes += [(cap, columns), (extra // 2, columns), (extra, columns)]
    return pl.pallas_call(
        functools.partial(compact_kernel, group, cap, extra, rows, shards, len(counts)),
        grid_spec=pltpu.PrefetchScalarGridSpec(
            num_scalar_prefetch=2,
            grid=(blocks // group,),
            in_specs=[pl.BlockSpec((1, group, BLOCK), lambda i, f, p: (i, 0, 0))]
            + [pl.BlockSpec((group * BLOCK, w), lambda i, f, p: (i, 0)) for w in (width, columns)]
            + [pl.BlockSpec(memory_space=pltpu.SMEM)] * len(counts),
            out_specs=[pl.BlockSpec(memory_space=pltpu.SMEM)]
            + [pl.BlockSpec(memory_space=pl.ANY)] * len(shapes),
            scratch_shapes=[
                pltpu.VMEM((rows, width), BF16),
                pltpu.VMEM((rows, columns), BF16),
                pltpu.SemaphoreType.DMA((shards + 5,)),
            ],
        ),
        out_shape=[jax.ShapeDtypeStruct((3,), jnp.int32)]
        + [jax.ShapeDtypeStruct(shape, BF16) for shape in shapes],
        compiler_params=pltpu.CompilerParams(vmem_limit_bytes=40 * MIB),
        cost_estimate=pl.CostEstimate(
            flops=2 * (BLOCK + SUB) * blocks * BLOCK * (width + columns),
            bytes_accessed=2 * (blocks * BLOCK + rows) * (width + columns),
            transcendentals=0,
        ),
        name="compact",
    )(firsts, pair_at.reshape(1), mask_blocks.reshape(-1, group, BLOCK), cells, targets, *counts)


SWAP = [(0, 1), (1, 0)]


def send(x, moves):
    return lax.ppermute(x, "tgt", moves)


def shifted(count, s, flip):
    return [(2 * z + y, 2 * ((z + s) % count) + (y ^ flip)) for z in range(count) for y in (0, 1)]


def latent_kernel(y_ref, slot_ref, cells_ref, factor_ref, out_ref):
    total = None
    for source in range(cells_ref.shape[0]):
        flip = (y_ref[0] + source) % 2
        part = dot(cells_ref[source], factor_ref[flip, slot_ref[source // 2]])
        total = part if total is None else total + part
    out_ref[...] = total.astype(BF16)


def latent_of(y, slot_of, cells, factor_in):
    sources, rows, width = cells.shape
    rank = factor_in.shape[3]
    return pl.pallas_call(
        latent_kernel,
        in_specs=[pl.BlockSpec(memory_space=pltpu.SMEM)] * 2 + [pl.BlockSpec(memory_space=pltpu.VMEM)] * 2,
        out_specs=pl.BlockSpec(memory_space=pltpu.VMEM),
        out_shape=jax.ShapeDtypeStruct((rows, rank), BF16),
        compiler_params=pltpu.CompilerParams(vmem_limit_bytes=16 * MIB),
        cost_estimate=pl.CostEstimate(
            flops=2 * sources * rows * width * rank,
            bytes_accessed=2 * sources * width * (rows + rank) + 2 * rows * rank,
            transcendentals=0,
        ),
        name="latent",
    )(y.reshape(1), slot_of, cells, factor_in)


def residual_kernel(
    count, mixed, own_ref, pair_ref, part_ref, scale_ref, weight_ref, far_weight_ref, factor_ref, far_factor_ref, *refs
):
    slot = pl.program_id(0)
    latents, refs = refs[:count], refs[count:]
    targets_ref, far_targets_ref, refs = refs[0], refs[1], refs[2:]
    if mixed:
        other_ref, first_ref, first_far_ref, refs = *refs[:3], refs[3:]
    terms, (out_ref, far_out_ref, held, *sums) = refs[:count], refs[count:]
    total_ref, far_total_ref = sums if mixed else (out_ref, far_out_ref)
    rows = targets_ref.shape[0]

    for s in range(count):

        @pl.when(slot == s)
        def _():
            held[...] = latents[s][...]

    @pl.when(slot == 0)
    def _():
        total_ref[...] = first_ref[...] if mixed else jnp.zeros_like(total_ref)
        far_total_ref[...] = first_far_ref[...] if mixed else jnp.zeros_like(far_total_ref)

    latent = held[...]
    targets = targets_ref[...].astype(F32)
    if mixed:
        row = own_ref[slot] * rows + lax.broadcasted_iota(jnp.int32, (rows, 1), 0)
        targets = jnp.where(row < part_ref[0], other_ref[...].astype(F32), targets)
    factor, far_factor = factor_ref[...], far_factor_ref[...]
    scale = scale_ref[0, 0]
    residual = ((dot(latent, factor) - targets) * scale * weight_ref[...]).astype(BF16)
    far_targets = far_targets_ref[...].astype(F32)
    far_residual = ((dot(latent, far_factor) - far_targets) * scale * far_weight_ref[...]).astype(BF16)
    total = dot(residual, factor, ((1,), (1,))) + dot(far_residual, far_factor, ((1,), (1,)))
    total = total.astype(BF16)
    for s in range(count):

        @pl.when(slot == s)
        def _():
            terms[s][...] = total

    total_ref[...] += dot(latent, residual, ((0,), (0,)))
    far_total_ref[...] += dot(latent, far_residual, ((0,), (0,)))
    if mixed:

        @pl.when(slot == count - 1)
        def _():
            half = total_ref.shape[0] // 2
            for out, at in ((out_ref, part_ref[1] * half), (far_out_ref, (1 - part_ref[1]) * half)):
                at = pl.multiple_of(at, half)
                out[0] = total_ref[pl.ds(at, half), :]
                out[1] = far_total_ref[pl.ds(at, half), :]


def residual_of(own_at, pair_at, part, scale, weights, factors, latents, own, pair, other=()):
    count = len(latents)
    rows, rank = latents[0].shape
    width = own.shape[1]
    mixed = len(other) > 0
    whole = lambda shape: pl.BlockSpec(shape, lambda i, o, p, r: (0,) * len(shape))
    out = (2, rank // 2, width) if mixed else (rank, width)
    by_own = pl.BlockSpec((rows, width), lambda i, o, p, r: (o[i], 0))
    by_pair = pl.BlockSpec((rows, width), lambda i, o, p, r: (p[i], 0))
    result = pl.pallas_call(
        functools.partial(residual_kernel, count, mixed),
        grid_spec=pltpu.PrefetchScalarGridSpec(
            num_scalar_prefetch=3,
            grid=(count,),
            in_specs=[pl.BlockSpec((1, 1), lambda i, o, p, r: (0, 0), memory_space=pltpu.SMEM)]
            + [whole((1, width))] * 2
            + [whole((rank, width))] * 2
            + [whole((rows, rank))] * count
            + [by_own, by_pair]
            + ([by_own] + [whole((rank, width))] * 2) * mixed,
            out_specs=[whole((rows, rank))] * count + [whole(out)] * 2,
            scratch_shapes=[pltpu.VMEM((rows, rank), BF16)] + [pltpu.VMEM((rank, width), F32)] * (2 * mixed),
        ),
        out_shape=[jax.ShapeDtypeStruct((rows, rank), BF16)] * count
        + [jax.ShapeDtypeStruct(out, F32)] * 2,
        compiler_params=pltpu.CompilerParams(vmem_limit_bytes=56 * MIB),
        cost_estimate=pl.CostEstimate(
            flops=count * rows * rank * width,
            bytes_accessed=count * rows * (rank + width),
            transcendentals=0,
        ),
        name="residual",
    )(
        own_at, pair_at, part, scale.reshape(1, 1), *[w.reshape(1, -1) for w in weights], *factors,
        *latents, own, pair, *other,
    )
    return result[:count], result[count], result[count + 1]


def in_kernel(tile_ref, *refs):
    (keep_ref, pass_ref), refs = refs[-2:], refs[:-2]
    half = keep_ref.shape[2]
    for tile in (0, 1):

        @pl.when(tile_ref[0] == tile)
        def _():
            for source in range(keep_ref.shape[0]):
                total = None
                for cells_ref, grads_ref in zip(refs[:CHUNKS], refs[CHUNKS:]):
                    part = dot(cells_ref[source], grads_ref[...], ((0,), (0,)))
                    total = part if total is None else total + part
                keep_ref[source] = total[:, tile * half : (tile + 1) * half]
                pass_ref[source] = total[:, (1 - tile) * half : (2 - tile) * half]


def in_of(tile, cells, latent_grads):
    sources, rows, width = cells[0].shape
    rank = latent_grads[0].shape[1]
    shape = jax.ShapeDtypeStruct((sources, width, rank // 2), F32)
    return pl.pallas_call(
        in_kernel,
        in_specs=[pl.BlockSpec(memory_space=pltpu.SMEM)]
        + [pl.BlockSpec(memory_space=pltpu.VMEM)] * (2 * CHUNKS),
        out_specs=[pl.BlockSpec(memory_space=pltpu.VMEM)] * 2,
        out_shape=[shape, shape],
        compiler_params=pltpu.CompilerParams(vmem_limit_bytes=16 * MIB),
        cost_estimate=pl.CostEstimate(
            flops=2 * CHUNKS * sources * rows * width * rank,
            bytes_accessed=2 * CHUNKS * rows * (width * sources + rank) + 4 * sources * width * rank,
            transcendentals=0,
        ),
        name="in_part",
    )(tile.reshape(1), *cells, *latent_grads)


def compacted_gradients(
    late, early, over, own_targets, pair_late, over_targets, received, whole_in, factors, weights, land_total
):
    shards = lax.axis_size("tgt")
    count = shards // 2
    index, tile = lax.axis_index("tgt"), lax.axis_index("tile")
    z, y = index // 2, index % 2
    extra = early.shape[0]
    scale = 1.0 / land_total
    slot_z = (z - jnp.arange(count, dtype=jnp.int32)) % count

    other_cells = lax.ppermute(over, "tile", SWAP)
    other_targets = lax.ppermute(over_targets, "tile", SWAP)

    def merged(own, other, at, size):
        row = at + lax.broadcasted_iota(jnp.int32, (size, 1), 0)
        own, other = (lax.dynamic_slice_in_dim(x, at, size, axis=0) for x in (own, other))
        return jnp.where(row < received[0], other, own)

    order = (1, 0)
    early = merged(early, other_cells, 0, extra)
    early = early.reshape(2, count, extra // shards, -1).swapaxes(0, 1).reshape(late.shape)

    def owners_cells(x):
        return lax.all_to_all(x, "tgt", split_axis=0, concat_axis=0, tiled=True)

    def along_line(x):
        return [x] + [send(x, shifted(count, s, 0)) for s in range(1, count)]

    pairs = {1: send(pair_late, shifted(count, 0, 1))}
    cells = {1: owners_cells(late), 0: owners_cells(early)}
    mine = latent_of(y, slot_z, cells[1], whole_in)
    mine, own_targets, other_targets = lax.optimization_barrier((mine, own_targets, other_targets))
    latents = {1: along_line(mine)}
    pair_early = merged(own_targets, other_targets, (1 - y) * (extra // 2), extra // 2)
    pairs[0] = send(pair_early, shifted(count, 0, 1))
    cells[0], latents[1] = lax.optimization_barrier((cells[0], latents[1]))
    latents[0] = along_line(latent_of(y, slot_z, cells[0], whole_in))

    def residual(chunk, *other):
        return residual_of(
            slot_z + (chunk * 2 + y) * count, slot_z, jnp.concatenate([received, tile.reshape(1)]),
            scale, weights, factors, latents[chunk], own_targets, pairs[chunk], other,
        )

    def summed(terms):
        total = terms[0].astype(F32)
        for s in range(1, count):
            total = total + send(terms[s], shifted(count, -s, 0)).astype(F32)
        return total.astype(BF16)

    late_parts, latents[0] = lax.optimization_barrier((residual(1), latents[0]))
    terms = list(late_parts[0])
    terms[count // 2], pairs[0] = lax.optimization_barrier((terms[count // 2], pairs[0]))
    grads = {1: summed(terms)}
    early_parts, grads[1] = lax.optimization_barrier(
        (residual(0, other_targets, *late_parts[1:]), grads[1])
    )
    grads[0] = summed(early_parts[0])
    out_half = early_parts[1] + lax.ppermute(early_parts[2], "tile", SWAP)
    grad_out = out_half[0] + send(out_half[1], shifted(count, 0, 1))
    grads[0], grad_out = lax.optimization_barrier((grads[0], grad_out))
    keep, passed = in_of(tile, [cells[c] for c in order], [grads[c] for c in order])
    mine = keep + lax.ppermute(passed, "tile", SWAP)
    grad_in = lax.dynamic_index_in_dim(mine, index, 0, keepdims=False)
    for s in range(1, shards):
        to_z, to_y = (z + s) % count, y ^ (s // count)
        part = lax.dynamic_index_in_dim(mine, 2 * to_z + to_y, 0, keepdims=False)
        grad_in = grad_in + send(part, shifted(count, s % count, s // count))
    return grad_in, grad_out


def full_gradients(cells, targets, factor_in, factor_out, target_weight, land_total):
    shards = lax.axis_size("tgt")
    own_cells = lax.all_to_all(cells, "tgt", split_axis=0, concat_axis=1, tiled=True)
    whole_in = lax.all_gather(factor_in, "tgt", axis=0, tiled=True)
    own_latent = dot(own_cells, whole_in).astype(BF16)
    latent = lax.all_gather(own_latent, "tgt", axis=0, tiled=True)
    residual = (
        (dot(latent, factor_out) - targets.astype(F32)) * (1.0 / land_total) * target_weight[None, :]
    ).astype(BF16)
    out_partial = dot(latent, residual, ((0,), (0,)))
    grad_out = lax.psum_scatter(out_partial, "tile", scatter_dimension=0, tiled=True)
    terms = dot(residual, factor_out, ((1,), (1,))).astype(BF16)
    parts = lax.all_to_all(
        terms.reshape(shards, -1, terms.shape[1]), "tgt", split_axis=0, concat_axis=0, tiled=True
    )
    latent_grad = jnp.sum(parts.astype(F32), axis=0).astype(BF16)
    in_partial = dot(own_cells, latent_grad, ((0,), (0,)))
    in_half = lax.psum_scatter(in_partial, "tile", scatter_dimension=1, tiled=True)
    grad_in = lax.psum_scatter(in_half, "tgt", scatter_dimension=0, tiled=True)
    return grad_in, grad_out


def local(embeddings, land_mask, factor_in, factor_out, targets, target_weight):
    cells = embeddings.shape[0]
    shards, groups = lax.axis_size("tgt"), lax.axis_size("groups")
    grain = SUB * shards * CHUNKS
    cap = -(-cells * 33 // (64 * grain)) * grain
    extra = cap // 2

    y = lax.axis_index("tgt") % 2
    pair_in = jnp.stack([factor_in, send(factor_in, shifted(shards // 2, 0, 1))])
    weights = (target_weight, send(target_weight, shifted(shards // 2, 0, 1)))
    mask_blocks = land_mask.reshape(-1, BLOCK)
    in_block = jnp.sum(mask_blocks, axis=1)
    land = jnp.sum(land_mask).reshape(1)
    at = jnp.arange(in_block.shape[0], dtype=jnp.int32)
    firsts = jnp.maximum(cap - land, 0) + jnp.sum(
        jnp.where(at[None, :] < at[:, None], in_block[None, :], 0), axis=1
    )
    counts = []
    for g in range(groups):
        for t in (0, 1):
            moves = [(2 * a + b, (a + g) % groups * 2 + (b ^ t)) for a in range(groups) for b in (0, 1)]
            counts.append(lax.ppermute(land, ("groups", "tile"), moves) if g + t else land)
    firsts, mask_blocks, counts, pair_in, weights = lax.optimization_barrier(
        (firsts, mask_blocks, counts, pair_in, weights)
    )
    line_in = [pair_in] + [send(pair_in, shifted(shards // 2, s, 0)) for s in range(1, shards // 2)]
    factors = (factor_out, send(factor_out, shifted(shards // 2, 0, 1)))
    facts, *kept = compact(
        firsts, extra + (1 - y) * (extra // 2), mask_blocks, embeddings, targets, counts, cap, extra, shards
    )
    facts, kept, line_in, factors = lax.optimization_barrier((facts, kept, line_in, factors))

    def few():
        return compacted_gradients(
            *kept, facts[1:2], jnp.stack(line_in, axis=1), factors, weights, facts[2].astype(F32)
        )

    def full():
        is_land = land_mask[:, None] > 0
        return full_gradients(
            jnp.where(is_land, embeddings, 0), jnp.where(is_land, targets, 0),
            factor_in, factor_out, target_weight, facts[2].astype(F32),
        )

    return lax.cond(facts[0] > 0, few, full)


def solution(mesh):
    return jax.shard_map(
        local,
        mesh=mesh,
        in_specs=(
            P(("groups", "tile"), "tgt"),
            P(("groups", "tile")),
            P("tgt", None),
            P(None, "tgt"),
            P(("groups", "tile"), "tgt"),
            P("tgt"),
        ),
        out_specs=(P(("groups", "tgt"), "tile"), P(("groups", "tile"), "tgt")),
        check_vma=False,
    )
```

```python
import functools

import jax
import jax.numpy as jnp
from jax import lax
from jax.experimental import pallas as pl
from jax.experimental.pallas import tpu as pltpu
from jax.sharding import PartitionSpec as P

BF16 = jnp.bfloat16
F32 = jnp.float32
BLOCK = 256
GROUP = 13
SUB = 16
CHUNKS = 2
MIB = 1024 * 1024


def dot(a, b, dims=((1,), (0,))):
    return lax.dot_general(a, b, (dims, ((), ())), preferred_element_type=F32)


def compact_kernel(
    group, cap, extra, rows, shards, known, plan_ref, mask_ref, cells_ref, targets_ref, *refs
):
    blocks = mask_ref.shape[0]
    (facts_ref, late_ref, early_ref, over_ref, main_ref, pair_out_ref, far_ref, cells_all, targets_all, place_in, sems) = refs
    step = pl.program_id(0)
    arrays = ((cells_ref, cells_all), (targets_ref, targets_all))

    @pl.when(step == 0)
    def _():
        counts = [plan_ref[blocks + i] for i in range(known)]
        fits = jnp.int32(1)
        for one, two in zip(counts[::2], counts[1::2]):
            low, high = jnp.minimum(one, two), jnp.maximum(one, two)
            fits = jnp.where((low + jnp.maximum(high - cap, 0) <= cap) & (high - cap <= extra), fits, 0)
        facts_ref[0] = fits
        facts_ref[1] = jnp.maximum(counts[1] - cap, 0)
        facts_ref[2] = counts[0] + counts[1]

        def clear(i, carry):
            for _, out_ref in arrays:
                out_ref[pl.ds(pl.multiple_of(i * BLOCK, BLOCK), BLOCK), :] = jnp.zeros(
                    (BLOCK, out_ref.shape[1]), out_ref.dtype
                )
            return carry

        lax.fori_loop(0, plan_ref[0] // BLOCK + 1, clear, 0)
        before = lax.broadcasted_iota(jnp.int32, (BLOCK, BLOCK), 0) < lax.broadcasted_iota(
            jnp.int32, (BLOCK, BLOCK), 1
        )
        before = before.astype(F32).astype(BF16)
        mask = mask_ref[...]
        prefix = dot(mask.astype(F32).astype(BF16), before).astype(jnp.int32)
        place_in[...] = jnp.where(mask > 0, prefix, -rows)

    place = lax.broadcasted_iota(jnp.int32, (BLOCK + SUB, BLOCK), 0)
    for k in range(group):
        first = plan_ref[step * group + k]
        start = jnp.minimum(first // SUB * SUB, rows - BLOCK - SUB)
        offset = jnp.minimum(first - start, rows - 1)
        slot = place_in[pl.ds(step * group + k, 1), :] + offset
        choose = (place == slot).astype(F32).astype(BF16)
        start = pl.multiple_of(start, SUB)
        for x_ref, out_ref in arrays:
            moved = dot(choose, x_ref[k * BLOCK : (k + 1) * BLOCK, :]).astype(BF16)
            out_ref[pl.ds(start, SUB), :] += moved[:SUB]
            out_ref[pl.ds(start + SUB, BLOCK), :] = moved[SUB:]

    @pl.when(step == pl.num_programs(0) - 1)
    def _():
        block, count = extra // shards, shards // 2
        moves = [
            (cells_all.at[pl.ds(extra + (y * count + z) * block, block)], late_ref.at[2 * z + y])
            for z in range(count)
            for y in (0, 1)
        ]
        moves += [
            (cells_all.at[pl.ds(cap, extra)], over_ref),
            (cells_all.at[pl.ds(0, extra)], early_ref),
            (targets_all.at[pl.ds(pl.multiple_of(plan_ref[blocks + known], SUB), extra // 2)], pair_out_ref),
            (targets_all.at[pl.ds(cap, extra)], far_ref),
            (targets_all.at[pl.ds(0, cap)], main_ref),
        ]
        copies = [pltpu.make_async_copy(x, out, sems.at[i]) for i, (x, out) in enumerate(moves)]
        for copy in copies:
            copy.start()
        for copy in copies:
            copy.wait()


def compact(firsts, pair_at, mask_blocks, cells, targets, counts, cap, extra, shards):
    rows = -(-(cap + extra + 2 * BLOCK) // BLOCK) * BLOCK
    blocks = mask_blocks.shape[0]
    group = max(g for g in range(1, GROUP + 1) if blocks % g == 0)
    at = jnp.arange(firsts.shape[0], dtype=jnp.int32)
    plan = jnp.where(at < blocks, firsts, pair_at)
    for i, known in enumerate(counts):
        plan = jnp.where(at == blocks + i, known, plan)
    width, columns = cells.shape[1], targets.shape[1]
    shapes = [(shards, extra // shards, width), (extra, width), (extra, width)]
    shapes += [(cap, columns), (extra // 2, columns), (extra, columns)]
    return pl.pallas_call(
        functools.partial(compact_kernel, group, cap, extra, rows, shards, len(counts)),
        grid_spec=pltpu.PrefetchScalarGridSpec(
            num_scalar_prefetch=1,
            grid=(blocks // group,),
            in_specs=[pl.BlockSpec((blocks, BLOCK), lambda i, p: (0, 0))]
            + [pl.BlockSpec((group * BLOCK, w), lambda i, p: (i, 0)) for w in (width, columns)],
            out_specs=[pl.BlockSpec(memory_space=pltpu.SMEM)]
            + [pl.BlockSpec(memory_space=pl.ANY)] * len(shapes),
            scratch_shapes=[
                pltpu.VMEM((rows, width), BF16),
                pltpu.VMEM((rows, columns), BF16),
                pltpu.VMEM((blocks, BLOCK), jnp.int32),
                pltpu.SemaphoreType.DMA((shards + 5,)),
            ],
        ),
        out_shape=[jax.ShapeDtypeStruct((3,), jnp.int32)]
        + [jax.ShapeDtypeStruct(shape, BF16) for shape in shapes],
        compiler_params=pltpu.CompilerParams(vmem_limit_bytes=40 * MIB),
        cost_estimate=pl.CostEstimate(
            flops=2 * (BLOCK + SUB) * blocks * BLOCK * (width + columns),
            bytes_accessed=2 * (blocks * BLOCK + rows) * (width + columns),
            transcendentals=0,
        ),
        name="compact",
    )(plan, mask_blocks, cells, targets)


SWAP = [(0, 1), (1, 0)]


def send(x, moves):
    return lax.ppermute(x, "tgt", moves)


def shifted(count, s, flip):
    return [(2 * z + y, 2 * ((z + s) % count) + (y ^ flip)) for z in range(count) for y in (0, 1)]


def latent_kernel(y_ref, slot_ref, cells_ref, factor_ref, out_ref):
    total = None
    for source in range(cells_ref.shape[0]):
        flip = (y_ref[0] + source) % 2
        part = dot(cells_ref[source], factor_ref[flip, slot_ref[source // 2]])
        total = part if total is None else total + part
    out_ref[...] = total.astype(BF16)


def latent_of(y, slot_of, cells, factor_in):
    sources, rows, width = cells.shape
    rank = factor_in.shape[3]
    return pl.pallas_call(
        latent_kernel,
        in_specs=[pl.BlockSpec(memory_space=pltpu.SMEM)] * 2 + [pl.BlockSpec(memory_space=pltpu.VMEM)] * 2,
        out_specs=pl.BlockSpec(memory_space=pltpu.VMEM),
        out_shape=jax.ShapeDtypeStruct((rows, rank), BF16),
        compiler_params=pltpu.CompilerParams(vmem_limit_bytes=16 * MIB),
        cost_estimate=pl.CostEstimate(
            flops=2 * sources * rows * width * rank,
            bytes_accessed=2 * sources * width * (rows + rank) + 2 * rows * rank,
            transcendentals=0,
        ),
        name="latent",
    )(y.reshape(1), slot_of, cells, factor_in)


def residual_kernel(
    count, mixed, own_ref, pair_ref, part_ref, scale_ref, weight_ref, far_weight_ref, factor_ref, far_factor_ref, *refs
):
    slot = pl.program_id(0)
    latents, refs = refs[:count], refs[count:]
    targets_ref, far_targets_ref, refs = refs[0], refs[1], refs[2:]
    if mixed:
        other_ref, first_ref, first_far_ref, refs = *refs[:3], refs[3:]
    terms, (out_ref, far_out_ref, held, *sums) = refs[:count], refs[count:]
    total_ref, far_total_ref = sums if mixed else (out_ref, far_out_ref)
    rows = targets_ref.shape[0]

    for s in range(count):

        @pl.when(slot == s)
        def _():
            held[...] = latents[s][...]

    @pl.when(slot == 0)
    def _():
        total_ref[...] = first_ref[...] if mixed else jnp.zeros_like(total_ref)
        far_total_ref[...] = first_far_ref[...] if mixed else jnp.zeros_like(far_total_ref)

    latent = held[...]
    targets = targets_ref[...].astype(F32)
    if mixed:
        row = own_ref[slot] * rows + lax.broadcasted_iota(jnp.int32, (rows, 1), 0)
        targets = jnp.where(row < part_ref[0], other_ref[...].astype(F32), targets)
    factor, far_factor = factor_ref[...], far_factor_ref[...]
    scale = scale_ref[0, 0]
    residual = ((dot(latent, factor) - targets) * scale * weight_ref[...]).astype(BF16)
    far_targets = far_targets_ref[...].astype(F32)
    far_residual = ((dot(latent, far_factor) - far_targets) * scale * far_weight_ref[...]).astype(BF16)
    total = dot(residual, factor, ((1,), (1,))) + dot(far_residual, far_factor, ((1,), (1,)))
    total = total.astype(BF16)
    for s in range(count):

        @pl.when(slot == s)
        def _():
            terms[s][...] = total

    total_ref[...] += dot(latent, residual, ((0,), (0,)))
    far_total_ref[...] += dot(latent, far_residual, ((0,), (0,)))
    if mixed:

        @pl.when(slot == count - 1)
        def _():
            half = total_ref.shape[0] // 2
            for out, at in ((out_ref, part_ref[1] * half), (far_out_ref, (1 - part_ref[1]) * half)):
                at = pl.multiple_of(at, half)
                out[0] = total_ref[pl.ds(at, half), :]
                out[1] = far_total_ref[pl.ds(at, half), :]


def residual_of(own_at, pair_at, part, scale, weights, factors, latents, own, pair, other=()):
    count = len(latents)
    rows, rank = latents[0].shape
    width = own.shape[1]
    mixed = len(other) > 0
    whole = lambda shape: pl.BlockSpec(shape, lambda i, o, p, r: (0,) * len(shape))
    out = (2, rank // 2, width) if mixed else (rank, width)
    by_own = pl.BlockSpec((rows, width), lambda i, o, p, r: (o[i], 0))
    by_pair = pl.BlockSpec((rows, width), lambda i, o, p, r: (p[i], 0))
    result = pl.pallas_call(
        functools.partial(residual_kernel, count, mixed),
        grid_spec=pltpu.PrefetchScalarGridSpec(
            num_scalar_prefetch=3,
            grid=(count,),
            in_specs=[pl.BlockSpec((1, 1), lambda i, o, p, r: (0, 0), memory_space=pltpu.SMEM)]
            + [whole((1, width))] * 2
            + [whole((rank, width))] * 2
            + [whole((rows, rank))] * count
            + [by_own, by_pair]
            + ([by_own] + [whole((rank, width))] * 2) * mixed,
            out_specs=[whole((rows, rank))] * count + [whole(out)] * 2,
            scratch_shapes=[pltpu.VMEM((rows, rank), BF16)] + [pltpu.VMEM((rank, width), F32)] * (2 * mixed),
        ),
        out_shape=[jax.ShapeDtypeStruct((rows, rank), BF16)] * count
        + [jax.ShapeDtypeStruct(out, F32)] * 2,
        compiler_params=pltpu.CompilerParams(vmem_limit_bytes=56 * MIB),
        cost_estimate=pl.CostEstimate(
            flops=count * rows * rank * width,
            bytes_accessed=count * rows * (rank + width),
            transcendentals=0,
        ),
        name="residual",
    )(
        own_at, pair_at, part, scale.reshape(1, 1), *[w.reshape(1, -1) for w in weights], *factors,
        *latents, own, pair, *other,
    )
    return result[:count], result[count], result[count + 1]


def in_kernel(tile_ref, *refs):
    (keep_ref, pass_ref), refs = refs[-2:], refs[:-2]
    half = keep_ref.shape[2]
    for tile in (0, 1):

        @pl.when(tile_ref[0] == tile)
        def _():
            for source in range(keep_ref.shape[0]):
                total = None
                for cells_ref, grads_ref in zip(refs[:CHUNKS], refs[CHUNKS:]):
                    part = dot(cells_ref[source], grads_ref[...], ((0,), (0,)))
                    total = part if total is None else total + part
                keep_ref[source] = total[:, tile * half : (tile + 1) * half]
                pass_ref[source] = total[:, (1 - tile) * half : (2 - tile) * half]


def in_of(tile, cells, latent_grads):
    sources, rows, width = cells[0].shape
    rank = latent_grads[0].shape[1]
    shape = jax.ShapeDtypeStruct((sources, width, rank // 2), F32)
    return pl.pallas_call(
        in_kernel,
        in_specs=[pl.BlockSpec(memory_space=pltpu.SMEM)]
        + [pl.BlockSpec(memory_space=pltpu.VMEM)] * (2 * CHUNKS),
        out_specs=[pl.BlockSpec(memory_space=pltpu.VMEM)] * 2,
        out_shape=[shape, shape],
        compiler_params=pltpu.CompilerParams(vmem_limit_bytes=16 * MIB),
        cost_estimate=pl.CostEstimate(
            flops=2 * CHUNKS * sources * rows * width * rank,
            bytes_accessed=2 * CHUNKS * rows * (width * sources + rank) + 4 * sources * width * rank,
            transcendentals=0,
        ),
        name="in_part",
    )(tile.reshape(1), *cells, *latent_grads)


def compacted_gradients(
    late, early, over, own_targets, pair_late, over_targets, received, whole_in, factors, weights, land_total
):
    shards = lax.axis_size("tgt")
    count = shards // 2
    index, tile = lax.axis_index("tgt"), lax.axis_index("tile")
    z, y = index // 2, index % 2
    extra = early.shape[0]
    scale = 1.0 / land_total
    slot_z = (z - jnp.arange(count, dtype=jnp.int32)) % count

    other_cells = lax.ppermute(over, "tile", SWAP)
    other_targets = lax.ppermute(over_targets, "tile", SWAP)

    def merged(own, other, at, size):
        row = at + lax.broadcasted_iota(jnp.int32, (size, 1), 0)
        own, other = (lax.dynamic_slice_in_dim(x, at, size, axis=0) for x in (own, other))
        return jnp.where(row < received[0], other, own)

    order = (1, 0)
    early = merged(early, other_cells, 0, extra)
    early = early.reshape(2, count, extra // shards, -1).swapaxes(0, 1).reshape(late.shape)

    def owners_cells(x):
        return lax.all_to_all(x, "tgt", split_axis=0, concat_axis=0, tiled=True)

    def along_line(x):
        return [x] + [send(x, shifted(count, s, 0)) for s in range(1, count)]

    pairs = {1: send(pair_late, shifted(count, 0, 1))}
    cells = {1: owners_cells(late), 0: owners_cells(early)}
    mine = latent_of(y, slot_z, cells[1], whole_in)
    mine, own_targets, other_targets = lax.optimization_barrier((mine, own_targets, other_targets))
    latents = {1: along_line(mine)}
    pair_early = merged(own_targets, other_targets, (1 - y) * (extra // 2), extra // 2)
    pairs[0] = send(pair_early, shifted(count, 0, 1))
    cells[0], latents[1] = lax.optimization_barrier((cells[0], latents[1]))
    latents[0] = along_line(latent_of(y, slot_z, cells[0], whole_in))

    def residual(chunk, *other):
        return residual_of(
            slot_z + (chunk * 2 + y) * count, slot_z, jnp.concatenate([received, tile.reshape(1)]),
            scale, weights, factors, latents[chunk], own_targets, pairs[chunk], other,
        )

    def summed(terms):
        total = terms[0].astype(F32)
        for s in range(1, count):
            total = total + send(terms[s], shifted(count, -s, 0)).astype(F32)
        return total.astype(BF16)

    late_parts, latents[0] = lax.optimization_barrier((residual(1), latents[0]))
    terms = list(late_parts[0])
    terms[1], pairs[0] = lax.optimization_barrier((terms[1], pairs[0]))
    grads = {1: summed(terms)}
    early_parts, grads[1] = lax.optimization_barrier(
        (residual(0, other_targets, *late_parts[1:]), grads[1])
    )
    grads[0] = summed(early_parts[0])
    out_half = early_parts[1] + lax.ppermute(early_parts[2], "tile", SWAP)
    grad_out = out_half[0] + send(out_half[1], shifted(count, 0, 1))
    grads[0], grad_out = lax.optimization_barrier((grads[0], grad_out))
    keep, passed = in_of(tile, [cells[c] for c in order], [grads[c] for c in order])
    mine = keep + lax.ppermute(passed, "tile", SWAP)
    grad_in = lax.dynamic_index_in_dim(mine, index, 0, keepdims=False)
    for s in range(1, shards):
        to_z, to_y = (z + s) % count, y ^ (s // count)
        part = lax.dynamic_index_in_dim(mine, 2 * to_z + to_y, 0, keepdims=False)
        grad_in = grad_in + send(part, shifted(count, s % count, s // count))
    return grad_in, grad_out


def full_gradients(cells, targets, factor_in, factor_out, target_weight, land_total):
    shards = lax.axis_size("tgt")
    own_cells = lax.all_to_all(cells, "tgt", split_axis=0, concat_axis=1, tiled=True)
    whole_in = lax.all_gather(factor_in, "tgt", axis=0, tiled=True)
    own_latent = dot(own_cells, whole_in).astype(BF16)
    latent = lax.all_gather(own_latent, "tgt", axis=0, tiled=True)
    residual = (
        (dot(latent, factor_out) - targets.astype(F32)) * (1.0 / land_total) * target_weight[None, :]
    ).astype(BF16)
    out_partial = dot(latent, residual, ((0,), (0,)))
    grad_out = lax.psum_scatter(out_partial, "tile", scatter_dimension=0, tiled=True)
    terms = dot(residual, factor_out, ((1,), (1,))).astype(BF16)
    parts = lax.all_to_all(
        terms.reshape(shards, -1, terms.shape[1]), "tgt", split_axis=0, concat_axis=0, tiled=True
    )
    latent_grad = jnp.sum(parts.astype(F32), axis=0).astype(BF16)
    in_partial = dot(own_cells, latent_grad, ((0,), (0,)))
    in_half = lax.psum_scatter(in_partial, "tile", scatter_dimension=1, tiled=True)
    grad_in = lax.psum_scatter(in_half, "tgt", scatter_dimension=0, tiled=True)
    return grad_in, grad_out


def local(embeddings, land_mask, factor_in, factor_out, targets, target_weight):
    cells = embeddings.shape[0]
    shards, groups = lax.axis_size("tgt"), lax.axis_size("groups")
    grain = SUB * shards * CHUNKS
    cap = -(-cells * 33 // (64 * grain)) * grain
    extra = cap // 2

    y = lax.axis_index("tgt") % 2
    pair_in = jnp.stack([factor_in, send(factor_in, shifted(shards // 2, 0, 1))])
    weights = (target_weight, send(target_weight, shifted(shards // 2, 0, 1)))
    mask_blocks = land_mask.reshape(-1, BLOCK)
    in_block = jnp.sum(mask_blocks, axis=1)
    land = jnp.sum(land_mask).reshape(1)
    at = jnp.arange(in_block.shape[0] + 2 * groups + 1, dtype=jnp.int32)
    firsts = jnp.maximum(cap - land, 0) + jnp.sum(
        jnp.where(at[None, : in_block.shape[0]] < at[:, None], in_block[None, :], 0), axis=1
    )
    counts = []
    for g in range(groups):
        for t in (0, 1):
            moves = [(2 * a + b, (a + g) % groups * 2 + (b ^ t)) for a in range(groups) for b in (0, 1)]
            counts.append(lax.ppermute(land, ("groups", "tile"), moves) if g + t else land)
    firsts, mask_blocks, counts, pair_in, weights = lax.optimization_barrier(
        (firsts, mask_blocks, counts, pair_in, weights)
    )
    line_in = [pair_in] + [send(pair_in, shifted(shards // 2, s, 0)) for s in range(1, shards // 2)]
    factors = (factor_out, send(factor_out, shifted(shards // 2, 0, 1)))
    facts, *kept = compact(
        firsts, extra + (1 - y) * (extra // 2), mask_blocks, embeddings, targets, counts, cap, extra, shards
    )
    facts, kept, line_in, factors = lax.optimization_barrier((facts, kept, line_in, factors))

    def few():
        return compacted_gradients(
            *kept, facts[1:2], jnp.stack(line_in, axis=1), factors, weights, facts[2].astype(F32)
        )

    def full():
        is_land = land_mask[:, None] > 0
        return full_gradients(
            jnp.where(is_land, embeddings, 0), jnp.where(is_land, targets, 0),
            factor_in, factor_out, target_weight, facts[2].astype(F32),
        )

    return lax.cond(facts[0] > 0, few, full)


def solution(mesh):
    return jax.shard_map(
        local,
        mesh=mesh,
        in_specs=(
            P(("groups", "tile"), "tgt"),
            P(("groups", "tile")),
            P("tgt", None),
            P(None, "tgt"),
            P(("groups", "tile"), "tgt"),
            P("tgt"),
        ),
        out_specs=(P(("groups", "tgt"), "tile"), P(("groups", "tile"), "tgt")),
        check_vma=False,
    )
```

```python
import functools

import jax
import jax.numpy as jnp
from jax import lax
from jax.experimental import pallas as pl
from jax.experimental.pallas import tpu as pltpu
from jax.sharding import PartitionSpec as P

BF16 = jnp.bfloat16
F32 = jnp.float32
BLOCK = 256
GROUP = 13
SUB = 16
CHUNKS = 2
MIB = 1024 * 1024


def dot(a, b, dims=((1,), (0,))):
    return lax.dot_general(a, b, (dims, ((), ())), preferred_element_type=F32)


def compact_kernel(
    group, cap, extra, rows, shards, known, plan_ref, mask_ref, cells_ref, targets_ref, *refs
):
    blocks = mask_ref.shape[0]
    (facts_ref, late_ref, early_ref, over_ref, main_ref, pair_out_ref, far_ref, cells_all, targets_all, place_in, sems) = refs
    step = pl.program_id(0)
    arrays = ((cells_ref, cells_all), (targets_ref, targets_all))

    @pl.when(step == 0)
    def _():
        counts = [plan_ref[blocks + i] for i in range(known)]
        fits = jnp.int32(1)
        for one, two in zip(counts[::2], counts[1::2]):
            low, high = jnp.minimum(one, two), jnp.maximum(one, two)
            fits = jnp.where((low + jnp.maximum(high - cap, 0) <= cap) & (high - cap <= extra), fits, 0)
        facts_ref[0] = fits
        facts_ref[1] = jnp.maximum(counts[1] - cap, 0)
        facts_ref[2] = counts[0] + counts[1]

        def clear(i, carry):
            for _, out_ref in arrays:
                out_ref[pl.ds(pl.multiple_of(i * BLOCK, BLOCK), BLOCK), :] = jnp.zeros(
                    (BLOCK, out_ref.shape[1]), out_ref.dtype
                )
            return carry

        lax.fori_loop(0, plan_ref[0] // BLOCK + 1, clear, 0)
        before = lax.broadcasted_iota(jnp.int32, (BLOCK, BLOCK), 0) < lax.broadcasted_iota(
            jnp.int32, (BLOCK, BLOCK), 1
        )
        before = before.astype(F32).astype(BF16)
        mask = mask_ref[...]
        prefix = dot(mask.astype(F32).astype(BF16), before).astype(jnp.int32)
        place_in[...] = jnp.where(mask > 0, prefix, -rows)

    place = lax.broadcasted_iota(jnp.int32, (BLOCK + SUB, BLOCK), 0)
    for k in range(group):
        first = plan_ref[step * group + k]
        start = jnp.minimum(first // SUB * SUB, rows - BLOCK - SUB)
        offset = jnp.minimum(first - start, rows - 1)
        slot = place_in[pl.ds(step * group + k, 1), :] + offset
        choose = (place == slot).astype(F32).astype(BF16)
        start = pl.multiple_of(start, SUB)
        for x_ref, out_ref in arrays:
            moved = dot(choose, x_ref[k * BLOCK : (k + 1) * BLOCK, :]).astype(BF16)
            out_ref[pl.ds(start, SUB), :] += moved[:SUB]
            out_ref[pl.ds(start + SUB, BLOCK), :] = moved[SUB:]

    @pl.when(step == pl.num_programs(0) - 1)
    def _():
        block, count = extra // shards, shards // 2
        moves = [
            (cells_all.at[pl.ds(extra + (y * count + z) * block, block)], late_ref.at[2 * z + y])
            for z in range(count)
            for y in (0, 1)
        ]
        moves += [
            (cells_all.at[pl.ds(cap, extra)], over_ref),
            (cells_all.at[pl.ds(0, extra)], early_ref),
            (targets_all.at[pl.ds(pl.multiple_of(plan_ref[blocks + known], SUB), extra // 2)], pair_out_ref),
            (targets_all.at[pl.ds(cap, extra)], far_ref),
            (targets_all.at[pl.ds(0, cap)], main_ref),
        ]
        copies = [pltpu.make_async_copy(x, out, sems.at[i]) for i, (x, out) in enumerate(moves)]
        for copy in copies:
            copy.start()
        for copy in copies:
            copy.wait()


def compact(firsts, pair_at, mask_blocks, cells, targets, counts, cap, extra, shards):
    rows = -(-(cap + extra + 2 * BLOCK) // BLOCK) * BLOCK
    blocks = mask_blocks.shape[0]
    group = max(g for g in range(1, GROUP + 1) if blocks % g == 0)
    at = jnp.arange(firsts.shape[0], dtype=jnp.int32)
    plan = jnp.where(at < blocks, firsts, pair_at)
    for i, known in enumerate(counts):
        plan = jnp.where(at == blocks + i, known, plan)
    width, columns = cells.shape[1], targets.shape[1]
    shapes = [(shards, extra // shards, width), (extra, width), (extra, width)]
    shapes += [(cap, columns), (extra // 2, columns), (extra, columns)]
    return pl.pallas_call(
        functools.partial(compact_kernel, group, cap, extra, rows, shards, len(counts)),
        grid_spec=pltpu.PrefetchScalarGridSpec(
            num_scalar_prefetch=1,
            grid=(blocks // group,),
            in_specs=[pl.BlockSpec((blocks, BLOCK), lambda i, p: (0, 0))]
            + [pl.BlockSpec((group * BLOCK, w), lambda i, p: (i, 0)) for w in (width, columns)],
            out_specs=[pl.BlockSpec(memory_space=pltpu.SMEM)]
            + [pl.BlockSpec(memory_space=pl.ANY)] * len(shapes),
            scratch_shapes=[
                pltpu.VMEM((rows, width), BF16),
                pltpu.VMEM((rows, columns), BF16),
                pltpu.VMEM((blocks, BLOCK), jnp.int32),
                pltpu.SemaphoreType.DMA((shards + 5,)),
            ],
        ),
        out_shape=[jax.ShapeDtypeStruct((3,), jnp.int32)]
        + [jax.ShapeDtypeStruct(shape, BF16) for shape in shapes],
        compiler_params=pltpu.CompilerParams(vmem_limit_bytes=40 * MIB),
        cost_estimate=pl.CostEstimate(
            flops=2 * (BLOCK + SUB) * blocks * BLOCK * (width + columns),
            bytes_accessed=2 * (blocks * BLOCK + rows) * (width + columns),
            transcendentals=0,
        ),
        name="compact",
    )(plan, mask_blocks, cells, targets)


SWAP = [(0, 1), (1, 0)]


def send(x, moves):
    return lax.ppermute(x, "tgt", moves)


def shifted(count, s, flip):
    return [(2 * z + y, 2 * ((z + s) % count) + (y ^ flip)) for z in range(count) for y in (0, 1)]


def latent_kernel(y_ref, slot_ref, cells_ref, factor_ref, out_ref):
    total = None
    for source in range(cells_ref.shape[0]):
        flip = (y_ref[0] + source) % 2
        part = dot(cells_ref[source], factor_ref[flip, slot_ref[source // 2]])
        total = part if total is None else total + part
    out_ref[...] = total.astype(BF16)


def latent_of(y, slot_of, cells, factor_in):
    sources, rows, width = cells.shape
    rank = factor_in.shape[3]
    return pl.pallas_call(
        latent_kernel,
        in_specs=[pl.BlockSpec(memory_space=pltpu.SMEM)] * 2 + [pl.BlockSpec(memory_space=pltpu.VMEM)] * 2,
        out_specs=pl.BlockSpec(memory_space=pltpu.VMEM),
        out_shape=jax.ShapeDtypeStruct((rows, rank), BF16),
        compiler_params=pltpu.CompilerParams(vmem_limit_bytes=16 * MIB),
        cost_estimate=pl.CostEstimate(
            flops=2 * sources * rows * width * rank,
            bytes_accessed=2 * sources * width * (rows + rank) + 2 * rows * rank,
            transcendentals=0,
        ),
        name="latent",
    )(y.reshape(1), slot_of, cells, factor_in)


def residual_kernel(
    count, mixed, own_ref, pair_ref, part_ref, scale_ref, weight_ref, far_weight_ref, factor_ref, far_factor_ref, *refs
):
    slot = pl.program_id(0)
    latents, refs = refs[:count], refs[count:]
    targets_ref, far_targets_ref, refs = refs[0], refs[1], refs[2:]
    if mixed:
        other_ref, first_ref, first_far_ref, refs = *refs[:3], refs[3:]
    terms, (out_ref, far_out_ref, held, *sums) = refs[:count], refs[count:]
    total_ref, far_total_ref = sums if mixed else (out_ref, far_out_ref)
    rows = targets_ref.shape[0]

    for s in range(count):

        @pl.when(slot == s)
        def _():
            held[...] = latents[s][...]

    @pl.when(slot == 0)
    def _():
        total_ref[...] = first_ref[...] if mixed else jnp.zeros_like(total_ref)
        far_total_ref[...] = first_far_ref[...] if mixed else jnp.zeros_like(far_total_ref)

    latent = held[...]
    targets = targets_ref[...].astype(F32)
    if mixed:
        row = own_ref[slot] * rows + lax.broadcasted_iota(jnp.int32, (rows, 1), 0)
        targets = jnp.where(row < part_ref[0], other_ref[...].astype(F32), targets)
    factor, far_factor = factor_ref[...], far_factor_ref[...]
    scale = scale_ref[0, 0]
    residual = ((dot(latent, factor) - targets) * scale * weight_ref[...]).astype(BF16)
    far_targets = far_targets_ref[...].astype(F32)
    far_residual = ((dot(latent, far_factor) - far_targets) * scale * far_weight_ref[...]).astype(BF16)
    total = dot(residual, factor, ((1,), (1,))) + dot(far_residual, far_factor, ((1,), (1,)))
    total = total.astype(BF16)
    for s in range(count):

        @pl.when(slot == s)
        def _():
            terms[s][...] = total

    total_ref[...] += dot(latent, residual, ((0,), (0,)))
    far_total_ref[...] += dot(latent, far_residual, ((0,), (0,)))
    if mixed:

        @pl.when(slot == count - 1)
        def _():
            half = total_ref.shape[0] // 2
            for out, at in ((out_ref, part_ref[1] * half), (far_out_ref, (1 - part_ref[1]) * half)):
                at = pl.multiple_of(at, half)
                out[0] = total_ref[pl.ds(at, half), :]
                out[1] = far_total_ref[pl.ds(at, half), :]


def residual_of(own_at, pair_at, part, scale, weights, factors, latents, own, pair, other=()):
    count = len(latents)
    rows, rank = latents[0].shape
    width = own.shape[1]
    mixed = len(other) > 0
    whole = lambda shape: pl.BlockSpec(shape, lambda i, o, p, r: (0,) * len(shape))
    out = (2, rank // 2, width) if mixed else (rank, width)
    by_own = pl.BlockSpec((rows, width), lambda i, o, p, r: (o[i], 0))
    by_pair = pl.BlockSpec((rows, width), lambda i, o, p, r: (p[i], 0))
    result = pl.pallas_call(
        functools.partial(residual_kernel, count, mixed),
        grid_spec=pltpu.PrefetchScalarGridSpec(
            num_scalar_prefetch=3,
            grid=(count,),
            in_specs=[pl.BlockSpec((1, 1), lambda i, o, p, r: (0, 0), memory_space=pltpu.SMEM)]
            + [whole((1, width))] * 2
            + [whole((rank, width))] * 2
            + [whole((rows, rank))] * count
            + [by_own, by_pair]
            + ([by_own] + [whole((rank, width))] * 2) * mixed,
            out_specs=[whole((rows, rank))] * count + [whole(out)] * 2,
            scratch_shapes=[pltpu.VMEM((rows, rank), BF16)] + [pltpu.VMEM((rank, width), F32)] * (2 * mixed),
        ),
        out_shape=[jax.ShapeDtypeStruct((rows, rank), BF16)] * count
        + [jax.ShapeDtypeStruct(out, F32)] * 2,
        compiler_params=pltpu.CompilerParams(vmem_limit_bytes=56 * MIB),
        cost_estimate=pl.CostEstimate(
            flops=count * rows * rank * width,
            bytes_accessed=count * rows * (rank + width),
            transcendentals=0,
        ),
        name="residual",
    )(
        own_at, pair_at, part, scale.reshape(1, 1), *[w.reshape(1, -1) for w in weights], *factors,
        *latents, own, pair, *other,
    )
    return result[:count], result[count], result[count + 1]


def in_kernel(tile_ref, *refs):
    (keep_ref, pass_ref), refs = refs[-2:], refs[:-2]
    half = keep_ref.shape[2]
    for tile in (0, 1):

        @pl.when(tile_ref[0] == tile)
        def _():
            for source in range(keep_ref.shape[0]):
                total = None
                for cells_ref, grads_ref in zip(refs[:CHUNKS], refs[CHUNKS:]):
                    part = dot(cells_ref[source], grads_ref[...], ((0,), (0,)))
                    total = part if total is None else total + part
                keep_ref[source] = total[:, tile * half : (tile + 1) * half]
                pass_ref[source] = total[:, (1 - tile) * half : (2 - tile) * half]


def in_of(tile, cells, latent_grads):
    sources, rows, width = cells[0].shape
    rank = latent_grads[0].shape[1]
    shape = jax.ShapeDtypeStruct((sources, width, rank // 2), F32)
    return pl.pallas_call(
        in_kernel,
        in_specs=[pl.BlockSpec(memory_space=pltpu.SMEM)]
        + [pl.BlockSpec(memory_space=pltpu.VMEM)] * (2 * CHUNKS),
        out_specs=[pl.BlockSpec(memory_space=pltpu.VMEM)] * 2,
        out_shape=[shape, shape],
        compiler_params=pltpu.CompilerParams(vmem_limit_bytes=16 * MIB),
        cost_estimate=pl.CostEstimate(
            flops=2 * CHUNKS * sources * rows * width * rank,
            bytes_accessed=2 * CHUNKS * rows * (width * sources + rank) + 4 * sources * width * rank,
            transcendentals=0,
        ),
        name="in_part",
    )(tile.reshape(1), *cells, *latent_grads)


def compacted_gradients(
    late, early, over, own_targets, pair_late, over_targets, received, whole_in, factors, weights, land_total
):
    shards = lax.axis_size("tgt")
    count = shards // 2
    index, tile = lax.axis_index("tgt"), lax.axis_index("tile")
    z, y = index // 2, index % 2
    extra = early.shape[0]
    scale = 1.0 / land_total
    slot_z = (z - jnp.arange(count, dtype=jnp.int32)) % count

    other_cells = lax.ppermute(over, "tile", SWAP)
    other_targets = lax.ppermute(over_targets, "tile", SWAP)

    def merged(own, other, at, size):
        row = at + lax.broadcasted_iota(jnp.int32, (size, 1), 0)
        own, other = (lax.dynamic_slice_in_dim(x, at, size, axis=0) for x in (own, other))
        return jnp.where(row < received[0], other, own)

    order = (1, 0)
    early = merged(early, other_cells, 0, extra)
    early = early.reshape(2, count, extra // shards, -1).swapaxes(0, 1).reshape(late.shape)

    def owners_cells(x):
        return lax.all_to_all(x, "tgt", split_axis=0, concat_axis=0, tiled=True)

    def along_line(x):
        return [x] + [send(x, shifted(count, s, 0)) for s in range(1, count)]

    pairs = {1: send(pair_late, shifted(count, 0, 1))}
    cells = {1: owners_cells(late), 0: owners_cells(early)}
    mine = latent_of(y, slot_z, cells[1], whole_in)
    mine, own_targets, other_targets = lax.optimization_barrier((mine, own_targets, other_targets))
    latents = {1: along_line(mine)}
    pair_early = merged(own_targets, other_targets, (1 - y) * (extra // 2), extra // 2)
    pairs[0] = send(pair_early, shifted(count, 0, 1))
    cells[0], latents[1] = lax.optimization_barrier((cells[0], latents[1]))
    latents[0] = along_line(latent_of(y, slot_z, cells[0], whole_in))

    def residual(chunk, *other):
        return residual_of(
            slot_z + (chunk * 2 + y) * count, slot_z, jnp.concatenate([received, tile.reshape(1)]),
            scale, weights, factors, latents[chunk], own_targets, pairs[chunk], other,
        )

    def exchanged(terms):
        return [terms[0]] + [send(terms[s], shifted(count, -s, 0)) for s in range(1, count)]

    def summed(parts):
        total = parts[0].astype(F32)
        for part in parts[1:]:
            total = total + part.astype(F32)
        return total.astype(BF16)

    late_parts, latents[0] = lax.optimization_barrier((residual(1), latents[0]))
    terms = list(late_parts[0])
    terms[1], pairs[0] = lax.optimization_barrier((terms[1], pairs[0]))
    late_terms = exchanged(terms)
    early_parts, late_terms = lax.optimization_barrier(
        (residual(0, other_targets, *late_parts[1:]), late_terms)
    )
    grads = {0: summed(exchanged(early_parts[0])), 1: summed(late_terms)}
    out_half = early_parts[1] + lax.ppermute(early_parts[2], "tile", SWAP)
    grad_out = out_half[0] + send(out_half[1], shifted(count, 0, 1))
    grads[0], grad_out = lax.optimization_barrier((grads[0], grad_out))
    keep, passed = in_of(tile, [cells[c] for c in order], [grads[c] for c in order])
    mine = keep + lax.ppermute(passed, "tile", SWAP)
    grad_in = lax.dynamic_index_in_dim(mine, index, 0, keepdims=False)
    for s in range(1, shards):
        to_z, to_y = (z + s) % count, y ^ (s // count)
        part = lax.dynamic_index_in_dim(mine, 2 * to_z + to_y, 0, keepdims=False)
        grad_in = grad_in + send(part, shifted(count, s % count, s // count))
    return grad_in, grad_out


def full_gradients(cells, targets, factor_in, factor_out, target_weight, land_total):
    shards = lax.axis_size("tgt")
    own_cells = lax.all_to_all(cells, "tgt", split_axis=0, concat_axis=1, tiled=True)
    whole_in = lax.all_gather(factor_in, "tgt", axis=0, tiled=True)
    own_latent = dot(own_cells, whole_in).astype(BF16)
    latent = lax.all_gather(own_latent, "tgt", axis=0, tiled=True)
    residual = (
        (dot(latent, factor_out) - targets.astype(F32)) * (1.0 / land_total) * target_weight[None, :]
    ).astype(BF16)
    out_partial = dot(latent, residual, ((0,), (0,)))
    grad_out = lax.psum_scatter(out_partial, "tile", scatter_dimension=0, tiled=True)
    terms = dot(residual, factor_out, ((1,), (1,))).astype(BF16)
    parts = lax.all_to_all(
        terms.reshape(shards, -1, terms.shape[1]), "tgt", split_axis=0, concat_axis=0, tiled=True
    )
    latent_grad = jnp.sum(parts.astype(F32), axis=0).astype(BF16)
    in_partial = dot(own_cells, latent_grad, ((0,), (0,)))
    in_half = lax.psum_scatter(in_partial, "tile", scatter_dimension=1, tiled=True)
    grad_in = lax.psum_scatter(in_half, "tgt", scatter_dimension=0, tiled=True)
    return grad_in, grad_out


def local(embeddings, land_mask, factor_in, factor_out, targets, target_weight):
    cells = embeddings.shape[0]
    shards, groups = lax.axis_size("tgt"), lax.axis_size("groups")
    grain = SUB * shards * CHUNKS
    cap = -(-cells * 33 // (64 * grain)) * grain
    extra = cap // 2

    y = lax.axis_index("tgt") % 2
    pair_in = jnp.stack([factor_in, send(factor_in, shifted(shards // 2, 0, 1))])
    weights = (target_weight, send(target_weight, shifted(shards // 2, 0, 1)))
    mask_blocks = land_mask.reshape(-1, BLOCK)
    in_block = jnp.sum(mask_blocks, axis=1)
    land = jnp.sum(land_mask).reshape(1)
    at = jnp.arange(in_block.shape[0] + 2 * groups + 1, dtype=jnp.int32)
    firsts = jnp.maximum(cap - land, 0) + jnp.sum(
        jnp.where(at[None, : in_block.shape[0]] < at[:, None], in_block[None, :], 0), axis=1
    )
    counts = []
    for g in range(groups):
        for t in (0, 1):
            moves = [(2 * a + b, (a + g) % groups * 2 + (b ^ t)) for a in range(groups) for b in (0, 1)]
            counts.append(lax.ppermute(land, ("groups", "tile"), moves) if g + t else land)
    firsts, mask_blocks, counts, pair_in, weights = lax.optimization_barrier(
        (firsts, mask_blocks, counts, pair_in, weights)
    )
    line_in = [pair_in] + [send(pair_in, shifted(shards // 2, s, 0)) for s in range(1, shards // 2)]
    factors = (factor_out, send(factor_out, shifted(shards // 2, 0, 1)))
    facts, *kept = compact(
        firsts, extra + (1 - y) * (extra // 2), mask_blocks, embeddings, targets, counts, cap, extra, shards
    )
    facts, kept, line_in, factors = lax.optimization_barrier((facts, kept, line_in, factors))

    def few():
        return compacted_gradients(
            *kept, facts[1:2], jnp.stack(line_in, axis=1), factors, weights, facts[2].astype(F32)
        )

    def full():
        is_land = land_mask[:, None] > 0
        return full_gradients(
            jnp.where(is_land, embeddings, 0), jnp.where(is_land, targets, 0),
            factor_in, factor_out, target_weight, facts[2].astype(F32),
        )

    return lax.cond(facts[0] > 0, few, full)


def solution(mesh):
    return jax.shard_map(
        local,
        mesh=mesh,
        in_specs=(
            P(("groups", "tile"), "tgt"),
            P(("groups", "tile")),
            P("tgt", None),
            P(None, "tgt"),
            P(("groups", "tile"), "tgt"),
            P("tgt"),
        ),
        out_specs=(P(("groups", "tgt"), "tile"), P(("groups", "tile"), "tgt")),
        check_vma=False,
    )
```
